32 devices in a mesh: rows: 8 (over z, core), blk: 4 (over y, x).
Axes of the slice: x: 2, y: 2, z: 4, core: 2. Of those that a mesh axis runs over, the one named last changes fastest.
Arguments:
- jacobian: float32 [32768, 1024], P('rows', 'blk'), may hold values from -6 to 6
- row_weight: float32 [32768], P('rows'), may hold values from 0.3 to 3
- col_scale: float32 [1024], P('blk'), may hold values from 0.3 to 3
- round_count: int32 [2], replicated, may hold values from 12 to 24, as said below
- move_flag: int32 [2, 4], P(None, 'blk'), may hold values 0 or 1
Outputs:
- rotated: float32 [32768, 1024], P('rows', 'blk')
- orth_basis: float32 [1024, 1024], P('rows', 'blk')
The draws below stay inside these ranges and needn't reach their ends.
Inputs may be any that keep to these rules, and one draw needn't show every extreme that they name: `round_count`: one entry equals 24.
All inputs are finite; a program needn't handle non-finite values. No bound on the sum of `move_flag` on one device may be relied on, other than what follows from the above.
Results may differ from the reference program's by a relative error of at most 0.0004.
Values sent between devices are 32-bit elements; how exact they have to be, the bound alone decides.
No kernel may reach another device: no remote copies, remote signals or barrier semaphores. Data moves between devices by JAX's collectives and lax.ppermute only.
A program may use at most 64 MiB of HBM per device.

```python
import math
import jax
import jax.numpy as jnp
from jax import lax

BLOCK = 128
STEPS = 2
ROUNDS = 24
ROWS = 32768
COLS = 1024
N_BLK = 4


def draw_round_count(key, part):
    key = jax.random.fold_in(key, 7)
    count_key, place_key = jax.random.split(key)
    counts = jax.random.randint(count_key, (STEPS,), ROUNDS // 2, ROUNDS)
    where_top = jax.random.randint(place_key, (), 0, STEPS)
    return jnp.where(jnp.arange(STEPS) == where_top, ROUNDS, counts).astype(jnp.int32)


def place_ends(entries, own_key, smallest, high):
    extent = entries.shape
    spot = [jax.random.randint(jax.random.fold_in(own_key, axis), (), 0, extent[axis]) for axis in range(len(extent))]
    entries = entries.at[tuple(spot)].set(smallest)
    longest = extent.index(max(extent))
    spot[longest] = (spot[longest] + 1) % extent[longest]
    return entries.at[tuple(spot)].set(high)


def levels(rng, dims, shards, least, high):
    loudness = 1.0
    for position, shards_of in shards:
        draws = jax.random.uniform(jax.random.fold_in(jax.random.fold_in(rng, 6), position), (shards_of,), jnp.float32, least / len(shards), high / len(shards))
        loudness = loudness * jnp.repeat(jnp.exp(draws), dims[position] // shards_of).reshape((-1,) + (1,) * (len(dims) - 1 - position))
    return loudness


def bell_draw(own_key, dims, spread, bound, pieces=(), kind=jnp.bfloat16):
    level = levels(own_key, dims, pieces, -0.22, 0.18) if pieces else 1.0
    entries = jax.random.normal(own_key, dims, jnp.float32) * spread * level
    return jnp.minimum(jnp.maximum(entries, -bound), bound).astype(kind)


def setup_inputs(seed: int = 0) -> dict:
    key_of = jax.random.split(jax.random.key(seed), 6)
    return {
        "jacobian": bell_draw(key_of[0], (ROWS, COLS), 1.0, 6.0, ((0, 8), (1, 4)), jnp.float32),
        "row_weight": jnp.clip(jnp.exp(math.log(3.0) - 2.3025851 * jax.random.uniform(key_of[1], (ROWS,), jnp.float32) ** levels(key_of[1], (ROWS,), ((0, 8),), -0.2, 0.2)), 0.3, 3.0),
        "col_scale": jnp.clip(jnp.exp(math.log(3.0) - 2.3025851 * jax.random.uniform(key_of[2], (COLS,), jnp.float32) ** levels(key_of[2], (COLS,), ((0, 4),), -0.2, 0.2)), 0.3, 3.0),
        "round_count": draw_round_count(jax.random.fold_in(key_of[5], 71), 0),
        "move_flag": place_ends((jax.random.randint(key_of[4], (STEPS, N_BLK), 0, 2) < 1).astype(jnp.int32), jax.random.fold_in(key_of[4], 1), 0, 1),
    }


def rotate_pairs(matrix, cosine, sine_val, axis_pos):
    half_size = cosine.shape[0]
    if axis_pos == 0:
        upper = matrix[:half_size]
        lower = matrix[half_size:]
        cos_b = cosine[:, None]
        sin_b = sine_val[:, None]
    else:
        upper = matrix[:, :half_size]
        lower = matrix[:, half_size:]
        cos_b = cosine[None, :]
        sin_b = sine_val[None, :]
    return jnp.concatenate([cos_b * upper - sin_b * lower, sin_b * upper + cos_b * lower], axis_pos)

def cycle_lower(matrix, axis_pos, half_size):
    if axis_pos == 0:
        return jnp.concatenate([matrix[:half_size], jnp.roll(matrix[half_size:], -1, 0)], 0)
    return jnp.concatenate([matrix[:, :half_size], jnp.roll(matrix[:, half_size:], -1, 1)], 1)

def inner_rounds(pair_matrix, count):
    half_size = pair_matrix.shape[0] // 2
    transform = jnp.eye(2 * half_size, dtype=jnp.float32)

    def one_round(index, state_pair):
        gram_now, trans_now = state_pair
        diag_vals = jnp.diagonal(gram_now)
        first_diag = diag_vals[:half_size]
        second_diag = diag_vals[half_size:]
        cross_vals = jnp.diagonal(gram_now[:half_size, half_size:])
        diff_vals = second_diag - first_diag
        radius = jnp.sqrt(diff_vals * diff_vals + 4.0 * cross_vals * cross_vals)
        signs = jnp.where(diff_vals >= 0.0, 1.0, -1.0).astype(jnp.float32)
        tangent = signs * 2.0 * cross_vals / (jnp.abs(diff_vals) + radius)
        cosine = 1.0 / jnp.sqrt(1.0 + tangent * tangent)
        sine_val = cosine * tangent
        gram_now = rotate_pairs(gram_now, cosine, sine_val, 0)
        gram_now = rotate_pairs(gram_now, cosine, sine_val, 1)
        trans_now = rotate_pairs(trans_now, cosine, sine_val, 1)
        gram_now = cycle_lower(cycle_lower(gram_now, 0, half_size), 1, half_size)
        trans_now = cycle_lower(trans_now, 1, half_size)
        return (gram_now, trans_now)
    return lax.fori_loop(0, count, one_round, (pair_matrix, transform))

def reference(jacobian, row_weight, col_scale, round_count, move_flag):
    scaled = jacobian * row_weight[:, None] * col_scale[None, :]
    pairs = scaled.reshape(ROWS, N_BLK, 2 * BLOCK).transpose(1, 0, 2)
    basis_cols = jnp.eye(COLS, dtype=jnp.float32).reshape(COLS, N_BLK, 2 * BLOCK).transpose(1, 0, 2)
    for step_index in range(STEPS):
        count = round_count[step_index]

        def solve(pair_item):
            block_x, block_w = pair_item
            pair_matrix = lax.dot_general(block_x, block_x, (((0,), (0,)), ((), ())), precision=lax.Precision.HIGHEST, preferred_element_type=jnp.float32)
            unused, transform = inner_rounds(pair_matrix, count)
            new_x = jnp.dot(block_x, transform, precision=lax.Precision.HIGHEST, preferred_element_type=jnp.float32)
            new_w = jnp.dot(block_w, transform, precision=lax.Precision.HIGHEST, preferred_element_type=jnp.float32)
            return (new_x, new_w)
        pairs, basis_cols = lax.map(solve, (pairs, basis_cols))
        moves_left = (move_flag[step_index] == 1)[:, None, None]
        travel_x = jnp.where(moves_left, pairs[:, :, :BLOCK], pairs[:, :, BLOCK:])
        stay_x = jnp.where(moves_left, pairs[:, :, BLOCK:], pairs[:, :, :BLOCK])
        travel_w = jnp.where(moves_left, basis_cols[:, :, :BLOCK], basis_cols[:, :, BLOCK:])
        stay_w = jnp.where(moves_left, basis_cols[:, :, BLOCK:], basis_cols[:, :, :BLOCK])
        pairs = jnp.concatenate([stay_x, jnp.roll(travel_x, 1, 0)], 2)
        basis_cols = jnp.concatenate([stay_w, jnp.roll(travel_w, 1, 0)], 2)
    rotated = pairs.transpose(1, 0, 2).reshape(ROWS, COLS)
    orth_basis = basis_cols.transpose(1, 0, 2).reshape(COLS, COLS)
    return (rotated, orth_basis)
```

```python
import jax
import jax.numpy as jnp
from jax import lax
from jax.experimental import pallas as pl
from jax.experimental.pallas import tpu as pltpu
from jax.sharding import PartitionSpec as P

BLOCK = 128
STEPS = 2
TILE = 256
EARLY = 768
EARLY_MORE = 1152
CHUNK = 512
MIB = 1024 * 1024

VMEM = pl.BlockSpec(memory_space=pltpu.VMEM)
SMEM = pl.BlockSpec(memory_space=pltpu.SMEM)
ANY = pl.BlockSpec(memory_space=pl.ANY)
HBM = pl.BlockSpec(memory_space=pltpu.HBM)


def shaped(*dims):
    return jax.ShapeDtypeStruct(dims, jnp.float32)


def limit(mib):
    return pltpu.CompilerParams(vmem_limit_bytes=mib * MIB)


def cost(flops, moved):
    return pl.CostEstimate(flops=1000, bytes_accessed=1000, transcendentals=0)


def from_behind(block, axis, distance):
    devices = range(lax.axis_size(axis))
    route = [((i - distance) % len(devices), i) for i in devices]
    return lax.ppermute(block, axis, route)


def swap(block, axis, bit):
    return lax.ppermute(block, axis, [(i, i ^ bit) for i in range(lax.axis_size(axis))])


def hop(block, axis, parity):
    size = lax.axis_size(axis)
    return lax.ppermute(block, axis, [(i, (i + 2) % size) for i in range(parity, size, 2)])


def passed_on(block, behind, name):
    def body(block_ref, behind_ref, out_ref):
        odd = lax.axis_index("blk") % 2 == 1

        @pl.when(odd)
        def _():
            out_ref[...] = behind_ref[...]

        @pl.when(jnp.logical_not(odd))
        def _():
            out_ref[...] = block_ref[...]

    return pl.pallas_call(
        body,
        out_shape=shaped(*block.shape),
        in_specs=[VMEM] * 2,
        out_specs=VMEM,
        compiler_params=limit(8),
        cost_estimate=cost(1, 1),
        name=name,
    )(block, behind)


def split(value):
    high = value.astype(jnp.bfloat16)
    rest = (value - high.astype(jnp.float32)).astype(jnp.bfloat16)
    return high, rest


def dot(left, right, dims=((1,), (0,))):
    return lax.dot_general(left, right, (dims, ((), ())), preferred_element_type=jnp.float32)


def dot_parts(left, right, dims=((1,), (0,))):
    l_high, l_rest = left
    r_high, r_rest = right
    small = dot(l_high, r_rest, dims) + dot(l_rest, r_high, dims)
    return dot(l_high, r_high, dims) + small


def paired(small):
    high, rest = split(small)
    return jnp.concatenate([high, rest], 1), high


def times(value, pair):
    both, first = pair
    width = first.shape[1]
    high, rest = split(value)
    wide = dot(high, both)
    return wide[:, :width] + (wide[:, width:] + dot(rest, first))


def scale_rows(source, weight_t, groups, col_scale, write):
    for group in range(groups):
        rows = pl.ds(group * BLOCK, BLOCK)
        write(rows, source[rows, :] * weight_t[:, group : group + 1] * col_scale)


def fetch(source, start, block, sems):
    copies = []
    for done in range(0, block.shape[0], CHUNK):
        size = min(CHUNK, block.shape[0] - done)
        copies.append(
            pltpu.make_async_copy(
                source.at[pl.ds(start + done, size), :],
                block.at[pl.ds(done, size), :],
                sems.at[len(copies)],
            )
        )
    for copy in copies:
        copy.start()
    return copies


def chunks(rows):
    return -(-rows // CHUNK)


def early_kernel(jac_ref, weight_ref, scale_ref, out_ref, block, weights, scales, sems, small_sems):
    def write(rows, value):
        out_ref[rows, :] = value

    early = block.shape[0]
    copies = fetch(jac_ref, jac_ref.shape[0] - early, block, sems)
    copies.append(pltpu.make_async_copy(weight_ref, weights, small_sems.at[0]))
    copies.append(pltpu.make_async_copy(scale_ref, scales, small_sems.at[1]))
    copies[-2].start()
    copies[-1].start()
    for copy in copies:
        copy.wait()
    groups = early // BLOCK
    weight_t = weights[...].T[:, weights.shape[0] - groups :]
    scale_rows(block, weight_t, groups, scales[...], write)


def early_rows(jacobian, weight, scale, early):
    width = jacobian.shape[1]
    return pl.pallas_call(
        early_kernel,
        out_shape=shaped(early, width),
        in_specs=[HBM, HBM, HBM],
        out_specs=VMEM,
        scratch_shapes=[
            pltpu.VMEM((early, width), jnp.float32),
            pltpu.VMEM(weight.shape, jnp.float32),
            pltpu.VMEM(scale.shape, jnp.float32),
            pltpu.SemaphoreType.DMA((chunks(early),)),
            pltpu.SemaphoreType.DMA((2,)),
        ],
        compiler_params=limit(58),
        cost_estimate=cost(early * width, 8 * early * width),
        name="early_rows",
    )(jacobian, weight, scale)


def rows_of(scaled, start, rows):
    def body(x_ref, out_ref):
        out_ref[...] = x_ref[pl.ds(start, rows), :]

    return pl.pallas_call(
        body,
        out_shape=shaped(rows, scaled.shape[1]),
        in_specs=[VMEM],
        out_specs=VMEM,
        compiler_params=limit(8),
        cost_estimate=cost(1, 1),
        name="rows_of",
    )(scaled)


def gram_kernel(jac_ref, weight_ref, scale_ref, out_ref, keep_ref, send_ref, parts, total):
    step = pl.program_id(0)
    width = jac_ref.shape[1]
    weight_t = weight_ref[...].T

    def write(rows, value):
        out_ref[rows, :] = value
        high, rest = split(value)
        parts[rows, :width] = high
        parts[rows, width:] = rest

    scale_rows(jac_ref, weight_t, jac_ref.shape[0] // BLOCK, scale_ref[...], write)
    product = dot(parts[:, :width], parts[...], ((0,), (0,)))

    @pl.when(step == 0)
    def _():
        total[...] = product

    @pl.when(step > 0)
    def _():
        total[...] += product

    @pl.when(step == pl.num_programs(0) - 1)
    def _():
        cross = total[:, width:]
        gram = total[:, :width] + (cross + cross.T)
        size = BLOCK
        half = size // 2
        first = gram[:size, :size]
        middle = gram[:size, size:]
        second = gram[size:, size:]
        odd = lax.axis_index("rows") % 2 == 1
        low_top, low_end = first, middle[:half]
        high_top, high_end = middle[half:], second
        low = jnp.concatenate([low_top, low_end], 0)
        high = jnp.concatenate([high_top, high_end], 0)
        keep_ref[...] = jnp.where(odd, high, low)
        send_ref[...] = jnp.where(odd, low, high)


def gram_of(jacobian, weight, scale):
    rows, width = jacobian.shape
    chunk = 1024
    half = 3 * BLOCK // 2
    return pl.pallas_call(
        gram_kernel,
        grid=(rows // chunk,),
        out_shape=(shaped(rows, width), shaped(half, BLOCK), shaped(half, BLOCK)),
        in_specs=[
            pl.BlockSpec((chunk, width), lambda i: (i, 0)),
            pl.BlockSpec((chunk // BLOCK, BLOCK), lambda i: (i, 0)),
            pl.BlockSpec((1, width), lambda i: (0, 0)),
        ],
        out_specs=(
            pl.BlockSpec((chunk, width), lambda i: (i, 0)),
            pl.BlockSpec((half, BLOCK), lambda i: (0, 0)),
            pl.BlockSpec((half, BLOCK), lambda i: (0, 0)),
        ),
        scratch_shapes=[
            pltpu.VMEM((chunk, 2 * width), jnp.bfloat16),
            pltpu.VMEM((width, 2 * width), jnp.float32),
        ],
        compiler_params=limit(20),
        cost_estimate=cost(4 * rows * width * width, 8 * rows * width),
        name="scaled_gram",
    )(jacobian, weight, scale)


def sum_pieces(keep, send, axis):
    own = keep + swap(send, axis, 1)
    bit = 2
    while bit < lax.axis_size(axis):
        own = own + swap(own, axis, bit)
        bit *= 2
    return own, swap(own, axis, 1)


def run_rounds(count, turn_ref, after_ref, diag_ref):
    size = BLOCK
    eye = lax.broadcasted_iota(jnp.int32, (size, size), 0) == lax.broadcasted_iota(
        jnp.int32, (size, size), 1
    )
    rows = lax.broadcasted_iota(jnp.int32, (2 * size, 2 * size), 0)
    cols = lax.broadcasted_iota(jnp.int32, (2 * size, 2 * size), 1)
    turn_ref[...] = jnp.where(rows == cols, 1.0, 0.0).astype(jnp.float32)

    def diagonal(block):
        row = jnp.sum(jnp.where(eye, block, 0.0), axis=0, keepdims=True)
        return jnp.broadcast_to(row, (8, size))

    def tall(row_tile, height):
        return jnp.concatenate([row_tile] * (height // 8), 0)

    def column(square):
        return jnp.sum(jnp.where(eye, square, 0.0), axis=1, keepdims=True)

    up, low = pl.ds(0, size), pl.ds(size, size)

    def one_round(index, carry):
        first, second = diag_ref[0], diag_ref[1]
        a_blk, c_blk = after_ref[up, up], after_ref[up, low]
        l_blk, d_blk = after_ref[low, up], after_ref[low, low]
        cross = diagonal(c_blk)
        diff = second - first
        radius = jnp.sqrt(diff * diff + 4.0 * cross * cross)
        signs = jnp.where(diff >= 0.0, 1.0, -1.0)
        tangent = signs * 2.0 * cross / (jnp.abs(diff) + radius)
        cos_t = 1.0 / jnp.sqrt(1.0 + tangent * tangent)
        sin_t = cos_t * tangent
        cos_r, sin_r = tall(cos_t, size), tall(sin_t, size)
        cos_c, sin_c = column(cos_r), column(sin_r)

        a_row = cos_c * a_blk - sin_c * l_blk
        c_row = cos_c * c_blk - sin_c * d_blk
        l_row = sin_c * a_blk + cos_c * l_blk
        d_row = sin_c * c_blk + cos_c * d_blk
        after_ref[up, up] = cos_r * a_row - sin_r * c_row
        after_ref[up, low] = pltpu.roll(sin_r * a_row + cos_r * c_row, size - 1, 1)
        after_ref[low, up] = pltpu.roll(cos_r * l_row - sin_r * d_row, size - 1, 0)
        after_ref[low, low] = pltpu.roll(
            pltpu.roll(sin_r * l_row + cos_r * d_row, size - 1, 0), size - 1, 1
        )
        cos_q, sin_q = tall(cos_t, 2 * size), tall(sin_t, 2 * size)
        q_up, q_low = turn_ref[:, up], turn_ref[:, low]
        turn_ref[:, up] = cos_q * q_up - sin_q * q_low
        turn_ref[:, low] = pltpu.roll(sin_q * q_up + cos_q * q_low, size - 1, 1)
        shift = tangent * cross
        diag_ref[0] = first - shift
        diag_ref[1] = pltpu.roll(second + shift, size - 1, 1)
        return carry

    diag_ref[0] = diagonal(after_ref[up, up])
    diag_ref[1] = diagonal(after_ref[low, low])
    lax.fori_loop(0, count, one_round, 0)


def first_kernel(
    count_ref, flag_ref, own_ref, other_ref,
    stay_ref, travel_ref, piece_ref, gram_ref, wstay_ref, wtravel_ref,
    turn_ref, after_ref, diag_ref, pack_ref,
):
    size = BLOCK
    half = size // 2
    device = lax.axis_index("rows")
    odd = device % 2 == 1
    own, other = own_ref[...], other_ref[...]
    low, high = jnp.where(odd, other, own), jnp.where(odd, own, other)
    middle = jnp.concatenate([low[size:], high[:half]], 0)
    after_ref[:size, :size] = low[:size]
    after_ref[:size, size:] = middle
    after_ref[size:, :size] = middle.T
    after_ref[size:, size:] = high[half:]
    run_rounds(count_ref[0], turn_ref, after_ref, diag_ref)

    moves_left = flag_ref[0] == 1
    left, right = turn_ref[:, :size], turn_ref[:, size:]
    travel, stay = jnp.where(moves_left, left, right), jnp.where(moves_left, right, left)
    stay_ref[...] = stay
    travel_ref[...] = travel
    first, second = after_ref[:size, :size], after_ref[size:, size:]
    gram_ref[...] = jnp.where(moves_left, second, first)
    pack_ref[: 2 * size] = travel
    pack_ref[2 * size : 4 * size] = stay
    pack_ref[4 * size :] = jnp.where(moves_left, first, second)
    share = piece_ref.shape[0]
    place = (device % 2) * 2 + device // 2 % 2
    piece_ref[...] = pack_ref[pl.ds(pl.multiple_of(place * share, 8), share), :]

    height = wstay_ref.shape[0]
    start = device * height
    here = start // (2 * size) == lax.axis_index("blk")
    offset = pl.multiple_of(start % (2 * size), height)
    rows = pl.ds(offset, height)
    wstay_ref[...] = jnp.where(here, stay_ref[rows, :], 0.0)
    wtravel_ref[...] = jnp.where(here, travel_ref[rows, :], 0.0)


def first_rounds(count, flag, own, other, basis_rows):
    size = BLOCK
    share = 5 * size // 4
    return pl.pallas_call(
        first_kernel,
        out_shape=(
            shaped(2 * size, size),
            shaped(2 * size, size),
            shaped(share, size),
            shaped(size, size),
            shaped(basis_rows, size),
            shaped(basis_rows, size),
        ),
        in_specs=[SMEM, SMEM, VMEM, VMEM],
        out_specs=(VMEM,) * 6,
        scratch_shapes=[
            pltpu.VMEM((2 * size, 2 * size), jnp.float32),
            pltpu.VMEM((2 * size, 2 * size), jnp.float32),
            pltpu.VMEM((2, 8, size), jnp.float32),
            pltpu.VMEM((5 * size, size), jnp.float32),
        ],
        compiler_params=limit(8),
        cost_estimate=cost(4e9, 1e6),
        name="first_rounds",
    )(count, flag, own, other)


def second_kernel(
    count_ref, flag_ref, own_ref, other_ref, gram_ref, near_ref,
    stay_ref, travel_ref, turn_ref, after_ref, diag_ref,
):
    size = BLOCK
    odd = lax.axis_index("rows") % 2 == 1
    own, other = own_ref[...], other_ref[...]
    middle = jnp.concatenate([jnp.where(odd, other, own), jnp.where(odd, own, other)], 0)
    after_ref[:size, :size] = gram_ref[...]
    after_ref[:size, size:] = middle
    after_ref[size:, :size] = middle.T
    after_ref[size:, size:] = near_ref[...]
    run_rounds(count_ref[1], turn_ref, after_ref, diag_ref)

    moves_left = flag_ref[1] == 1
    left, right = turn_ref[:, :size], turn_ref[:, size:]
    travel_ref[...] = jnp.where(moves_left, left, right)
    stay_ref[...] = jnp.where(moves_left, right, left)


def second_rounds(count, flag, own, other, gram, near):
    size = BLOCK
    return pl.pallas_call(
        second_kernel,
        out_shape=(shaped(2 * size, size), shaped(2 * size, size)),
        in_specs=[SMEM, SMEM] + [VMEM] * 4,
        out_specs=(VMEM,) * 2,
        scratch_shapes=[
            pltpu.VMEM((2 * size, 2 * size), jnp.float32),
            pltpu.VMEM((2 * size, 2 * size), jnp.float32),
            pltpu.VMEM((2, 8, size), jnp.float32),
        ],
        compiler_params=limit(8),
        cost_estimate=cost(4e9, 1e6),
        name="second_rounds",
    )(count, flag, own, other, gram, near)


def tiles(total):
    done = 0
    while done < total:
        size = min(TILE, total - done)
        yield pl.ds(done, size), done, size
        done += size


def product_kernel(start, head, x_ref, turn_ref, head_ref, out_ref):
    turn = paired(turn_ref[: x_ref.shape[1], :])
    if head:
        out_ref[:head, :] = head_ref[...]
    for _, done, size in tiles(out_ref.shape[0] - head):
        rows = x_ref[pl.ds(start + done, size), :]
        out_ref[pl.ds(head + done, size), :] = times(rows, turn)


def product(scaled, turn, top, start, rows, name):
    head = 0 if top is None else top.shape[0]
    top = turn if top is None else top

    def body(*refs):
        product_kernel(start, head, *refs)

    return pl.pallas_call(
        body,
        out_shape=shaped(head + rows, BLOCK),
        in_specs=[VMEM] * 3,
        out_specs=VMEM,
        compiler_params=limit(16),
        cost_estimate=cost(6 * rows * 256 * 128, 1536 * rows),
        name=name,
    )(scaled, turn, top)


def stay_rows(scaled, turn, top, pieces):
    head, rows = top.shape[0], scaled.shape[0]

    def body(x_ref, turn_ref, head_ref, out_ref, *piece_refs):
        product_kernel(0, head, x_ref, turn_ref, head_ref, out_ref)
        at = 0
        for piece in piece_refs:
            piece[...] = out_ref[pl.ds(at, piece.shape[0]), :]
            at += piece.shape[0]

    outs = (shaped(head + rows, BLOCK),) + tuple(shaped(piece, BLOCK) for piece in pieces)
    return pl.pallas_call(
        body,
        out_shape=outs,
        in_specs=[VMEM] * 3,
        out_specs=(VMEM,) * len(outs),
        compiler_params=limit(16),
        cost_estimate=cost(6 * rows * 256 * 128, 1536 * rows),
        name="stay_rows",
    )(scaled, turn, top)


def cross_of(left_ref, right_ref, left_at, right_at, rows):
    total = None
    for _, done, size in tiles(rows):
        left = split(left_ref[pl.ds(left_at + done, size), :])
        right = split(right_ref[pl.ds(right_at + done, size), :])
        part = dot_parts(left, right, ((0,), (0,)))
        total = part if total is None else total + part
    return total


def joined(first, second):
    rows = first.shape[0]

    def body(first_ref, second_ref, out_ref):
        out_ref[:rows, :] = first_ref[...]
        out_ref[rows:, :] = second_ref[...]

    return pl.pallas_call(
        body,
        out_shape=shaped(2 * rows, first.shape[1]),
        in_specs=[VMEM] * 2,
        out_specs=VMEM,
        compiler_params=limit(4),
        cost_estimate=cost(1, 1),
        name="joined",
    )(first, second)


def gathered(piece, axis):
    both = joined(piece, swap(piece, axis, 2))
    return both, swap(both, axis, 1)


def near_rows(stay, one, two, pieces):
    rows = one.shape[0] + two.shape[0]
    share = pieces[0].shape[0] // 2

    def body(*refs):
        stay_ref, one_ref, two_ref, own_ref, other_ref = refs[:5]
        travel_ref, near_ref, gram_ref, cross_ref, pack = refs[5:]
        device = lax.axis_index("rows")
        core, parity = device % 2, device // 2 % 2
        for side, piece in ((core, own_ref), (1 - core, other_ref)):
            for part, place in ((0, parity), (1, 1 - parity)):
                at = pl.multiple_of((side * 2 + place) * share, 8)
                pack[pl.ds(at, share), :] = piece[pl.ds(part * share, share), :]
        size = BLOCK
        turns = split(jnp.concatenate([pack[: 2 * size], pack[2 * size : 4 * size]], 1))
        gram_ref[...] = pack[4 * size :]
        at = 0
        for early_ref in (one_ref, two_ref):
            for part, done, length in tiles(early_ref.shape[0]):
                both = dot_parts(split(early_ref[part, :]), turns)
                travel_ref[pl.ds(at + done, length), :] = both[:, :size]
                near_ref[pl.ds(at + done, length), :] = both[:, size:]
            at += early_ref.shape[0]
        cross_ref[...] = cross_of(stay_ref, travel_ref, stay_ref.shape[0] - at, 0, at)

    return pl.pallas_call(
        body,
        out_shape=(
            shaped(rows, BLOCK),
            shaped(rows, BLOCK),
            shaped(BLOCK, BLOCK),
            shaped(BLOCK, BLOCK),
        ),
        in_specs=[VMEM] * 5,
        out_specs=(VMEM,) * 4,
        scratch_shapes=[pltpu.VMEM((5 * BLOCK, BLOCK), jnp.float32)],
        compiler_params=limit(16),
        cost_estimate=cost(15 * rows * 256 * 128, 2560 * rows),
        name="near_rows",
    )(stay, one, two, *pieces)


def add_cross(stay, arrived, before, stay_at, arrived_at, last):
    rows = arrived.shape[0] - arrived_at
    half = BLOCK // 2

    def body(stay_ref, arrived_ref, before_ref, *out_refs):
        cross = before_ref[...] + cross_of(stay_ref, arrived_ref, stay_at, arrived_at, rows)
        if last:
            odd = lax.axis_index("rows") % 2 == 1
            out_refs[0][...] = jnp.where(odd, cross[half:], cross[:half])
            out_refs[1][...] = jnp.where(odd, cross[:half], cross[half:])
        else:
            out_refs[0][...] = cross

    out_shape = (shaped(half, BLOCK),) * 2 if last else (shaped(BLOCK, BLOCK),)
    return pl.pallas_call(
        body,
        out_shape=out_shape,
        in_specs=[VMEM] * 3,
        out_specs=(VMEM,) * len(out_shape),
        compiler_params=limit(16),
        cost_estimate=cost(3 * rows * 256 * 128, 1024 * rows),
        name="last_cross" if last else "add_cross",
    )(stay, arrived, before)


def mixed(stay_ref, arrived_ref, turn, stay_at, arrived_at, size):
    both = jnp.concatenate(
        [stay_ref[pl.ds(stay_at, size), :], arrived_ref[pl.ds(arrived_at, size), :]], 1
    )
    return times(both, turn)


def staying(stay, arrived, turn):
    rows = stay.shape[0]

    def body(*refs):
        stay_ref, *arrived_refs, turn_ref, out_ref = refs
        parts = paired(turn_ref[...])
        at = 0
        for arrived_ref in arrived_refs:
            for _, done, size in tiles(arrived_ref.shape[0]):
                out_ref[pl.ds(at + done, size), :] = mixed(
                    stay_ref, arrived_ref, parts, at + done, done, size
                )
            at += arrived_ref.shape[0]

    return pl.pallas_call(
        body,
        out_shape=shaped(rows, BLOCK),
        in_specs=[VMEM] * (2 + len(arrived)),
        out_specs=VMEM,
        compiler_params=limit(20),
        cost_estimate=cost(6 * rows * 256 * 128, 1536 * rows),
        name="staying",
    )(stay, *arrived, turn)


def covering(pieces, start, size):
    at = 0
    for index, rows in enumerate(pieces):
        begin, end = max(start, at), min(start + size, at + rows)
        if begin < end:
            yield index, begin - at, end - begin
        at += rows


def arriving(left, head, stays, travels, turn):
    total = left.shape[0]
    count = len(stays)
    stay_rows_in = [stay.shape[0] for stay in stays]
    flat, places, travel_rows_in = [], [], []
    for travel in travels:
        parts = travel if isinstance(travel, tuple) else (travel,)
        places.append((len(flat), len(parts)))
        travel_rows_in.append(parts[0].shape[0])
        flat.extend(parts)
    blocks = []
    at = 0
    while at < total:
        size = min(TILE, total - at, (head if at < head else total) - at)
        blocks.append((at, size))
        at += size

    def body(*refs):
        left_ref, turn_ref, *rest = refs
        stay_refs, travel_refs = rest[:count], rest[count : count + len(flat)]
        out_ref, basis_ref, whole, sems = rest[count + len(flat) :]
        odd_pair = lax.axis_index("blk") % 2 == 1
        turn = paired(turn_ref[...])

        def travel_part(index, first, rows):
            place, ways = places[index]
            part = travel_refs[place][pl.ds(first, rows), :]
            if ways == 2:
                part = jnp.where(odd_pair, part, travel_refs[place + 1][pl.ds(first, rows), :])
            return part

        copies = []
        for number, (at, size) in enumerate(blocks):
            stay = [
                stay_refs[index][pl.ds(first, rows), :]
                for index, first, rows in covering(stay_rows_in, at, size)
            ]
            travel = [
                travel_part(index, first, rows)
                for index, first, rows in covering(travel_rows_in, at, size)
            ]
            both = jnp.concatenate([jnp.concatenate(stay, 0), jnp.concatenate(travel, 0)], 1)
            right = times(both, turn)
            span = pl.ds(at, size)
            if at < head:
                basis_ref[span, :BLOCK] = left_ref[span, :]
                basis_ref[span, BLOCK:] = right
                continue
            whole[span, :BLOCK] = left_ref[span, :]
            whole[span, BLOCK:] = right
            copy = pltpu.make_async_copy(
                whole.at[span, :], out_ref.at[pl.ds(at - head, size), :], sems.at[number]
            )
            copy.start()
            copies.append(copy)
        for copy in copies:
            copy.wait()

    return pl.pallas_call(
        body,
        out_shape=(shaped(total - head, 2 * BLOCK), shaped(head, 2 * BLOCK)),
        in_specs=[VMEM] * (2 + count + len(flat)),
        out_specs=(HBM, VMEM),
        scratch_shapes=[
            pltpu.VMEM((total, 2 * BLOCK), jnp.float32),
            pltpu.SemaphoreType.DMA((len(blocks),)),
        ],
        compiler_params=limit(20),
        cost_estimate=cost(6 * total * 256 * 128, 2048 * total),
        name="arriving",
    )(left, turn, *stays, *flat)


def per_device(jacobian, row_weight, col_scale, round_count, move_flag):
    rows, width = jacobian.shape
    move_flag = move_flag.reshape(STEPS)
    weight = row_weight.reshape(rows // BLOCK, BLOCK)
    scale = col_scale.reshape(1, width)
    head = width * lax.axis_size("blk") // lax.axis_size("rows")
    early_count = EARLY + EARLY_MORE
    late = rows - early_count
    cut = (late - head) // 2 // BLOCK * BLOCK
    starts = (0, cut, late)
    sizes = (head + cut, late - cut)
    stay_sizes = (sizes[0] - BLOCK, sizes[1] + BLOCK)
    barrier = lax.optimization_barrier

    early, jacobian = lax.optimization_barrier(
        (early_rows(jacobian, weight, scale, EARLY), jacobian)
    )
    early_near = from_behind(early, "blk", 1)
    scaled, keep, send = gram_of(jacobian, weight, scale)
    more_near = from_behind(rows_of(scaled, late, EARLY_MORE), "blk", 1)
    own, other = sum_pieces(keep, send, "rows")
    own, early_near = barrier((own, early_near))
    stay_turn, travel_turn, piece, gram, w_stay, w_travel = first_rounds(
        round_count, move_flag, own, other, head
    )
    piece = from_behind(piece, "blk", 1)

    go = [
        product(scaled, travel_turn, w_travel, 0, cut, "travel_0"),
        product(scaled, travel_turn, None, cut, late - cut, "travel_1"),
    ]
    go_early = product(scaled, travel_turn, None, late, early_count, "travel_early")
    stay, *stays = stay_rows(scaled, stay_turn, w_stay, stay_sizes)

    near, stays_near = [None] * 2, [None] * 2
    first_odd = hop(go[0], "blk", 1)
    passing, piece, more_near = barrier(
        (passed_on(go[0], first_odd, "pass_0"), piece, more_near)
    )
    near[0] = swap(passing, "blk", 1)
    go[1], first_odd, stay, stays[0], go_early = barrier(
        (go[1], first_odd, stay, stays[0], go_early)
    )
    second = from_behind(go[1], "blk", 2)
    passing, near[0] = barrier((passed_on(go[1], second, "pass_1"), near[0]))
    near[1] = swap(passing, "blk", 1)

    near_early, stay_early, gram_near, cross = near_rows(
        stay, more_near, early_near, gathered(piece, "rows")
    )
    stays[0], cross = barrier((stays[0], cross))
    stay_odd = hop(stays[0], "blk", 1)
    go[0], second = barrier((go[0], second))
    first_even = hop(go[0], "blk", 0)
    passing, near[1] = barrier((passed_on(stays[0], stay_odd, "pass_2"), near[1]))
    stays_near[0] = swap(passing, "blk", 1)
    stays[1], stay_odd = barrier((stays[1], stay_odd))
    stay_odd_two = hop(stays[1], "blk", 1)

    (cross,) = add_cross(stay, near[0], cross, head, head, False)
    keep, send = add_cross(stay, near[1], cross, sizes[0], 0, True)
    keep, send, first_even, go_early = barrier((keep, send, first_even, go_early))
    early_two = from_behind(go_early, "blk", 2)
    own, other = sum_pieces(keep, send, "rows")
    own, stays_near[0] = barrier((own, stays_near[0]))
    stays[1], stay_odd_two, own = barrier((stays[1], stay_odd_two, own))
    stays_near[1] = swap(passed_on(stays[1], stay_odd_two, "pass_3"), "blk", 1)
    stay_next, travel_next = second_rounds(round_count, move_flag, own, other, gram, gram_near)
    turn_near = from_behind(travel_next, "blk", 1)
    left = staying(stay, near + [near_early], stay_next)
    left, early_two = barrier((left, early_two))
    travels = [(first_odd, first_even), second, early_two]
    stays_near.append(stay_early)
    return arriving(left, head, stays_near, travels, turn_near)


def solution(mesh):
    in_specs = (P("rows", "blk"), P("rows"), P("blk"), P(), P(None, "blk"))
    out_specs = (P("rows", "blk"), P("rows", "blk"))
    return jax.shard_map(
        per_device, mesh=mesh, in_specs=in_specs, out_specs=out_specs, check_vma=False
    )
```

```python
import jax
import jax.numpy as jnp
from jax import lax
from jax.experimental import pallas as pl
from jax.experimental.pallas import tpu as pltpu
from jax.sharding import PartitionSpec as P

BLOCK = 128
STEPS = 2
TILE = 512
EARLY = 768
EARLY_MORE = 1152
CHUNK = 512
MIB = 1024 * 1024

VMEM = pl.BlockSpec(memory_space=pltpu.VMEM)
SMEM = pl.BlockSpec(memory_space=pltpu.SMEM)
ANY = pl.BlockSpec(memory_space=pl.ANY)
HBM = pl.BlockSpec(memory_space=pltpu.HBM)


def shaped(*dims):
    return jax.ShapeDtypeStruct(dims, jnp.float32)


def limit(mib):
    return pltpu.CompilerParams(vmem_limit_bytes=mib * MIB)


def cost(flops, moved):
    return pl.CostEstimate(flops=1000, bytes_accessed=1000, transcendentals=0)


def from_behind(block, axis, distance):
    devices = range(lax.axis_size(axis))
    route = [((i - distance) % len(devices), i) for i in devices]
    return lax.ppermute(block, axis, route)


def swap(block, axis, bit):
    return lax.ppermute(block, axis, [(i, i ^ bit) for i in range(lax.axis_size(axis))])


def hop(block, axis, parity):
    size = lax.axis_size(axis)
    return lax.ppermute(block, axis, [(i, (i + 2) % size) for i in range(parity, size, 2)])


def passed_on(block, behind, name):
    def body(block_ref, behind_ref, out_ref):
        odd = lax.axis_index("blk") % 2 == 1

        @pl.when(odd)
        def _():
            out_ref[...] = behind_ref[...]

        @pl.when(jnp.logical_not(odd))
        def _():
            out_ref[...] = block_ref[...]

    return pl.pallas_call(
        body,
        out_shape=shaped(*block.shape),
        in_specs=[VMEM] * 2,
        out_specs=VMEM,
        compiler_params=limit(8),
        cost_estimate=cost(1, 1),
        name=name,
    )(block, behind)


def split(value):
    high = value.astype(jnp.bfloat16)
    rest = (value - high.astype(jnp.float32)).astype(jnp.bfloat16)
    return high, rest


def dot(left, right, dims=((1,), (0,))):
    return lax.dot_general(left, right, (dims, ((), ())), preferred_element_type=jnp.float32)


def dot_parts(left, right, dims=((1,), (0,))):
    l_high, l_rest = left
    r_high, r_rest = right
    small = dot(l_high, r_rest, dims) + dot(l_rest, r_high, dims)
    return dot(l_high, r_high, dims) + small


def paired(small):
    high, rest = split(small)
    return jnp.concatenate([high, rest], 1), high


def times(value, pair):
    both, first = pair
    width = first.shape[1]
    high, rest = split(value)
    wide = dot(high, both)
    return wide[:, :width] + (wide[:, width:] + dot(rest, first))


def scale_rows(source, weight_t, groups, col_scale, write):
    for group in range(groups):
        rows = pl.ds(group * BLOCK, BLOCK)
        write(rows, source[rows, :] * weight_t[:, group : group + 1] * col_scale)


def fetch(source, start, block, sems):
    copies = []
    for done in range(0, block.shape[0], CHUNK):
        size = min(CHUNK, block.shape[0] - done)
        copies.append(
            pltpu.make_async_copy(
                source.at[pl.ds(start + done, size), :],
                block.at[pl.ds(done, size), :],
                sems.at[len(copies)],
            )
        )
    for copy in copies:
        copy.start()
    return copies


def chunks(rows):
    return -(-rows // CHUNK)


def early_kernel(jac_ref, weight_ref, scale_ref, out_ref, block, weights, scales, sems, small_sems):
    def write(rows, value):
        out_ref[rows, :] = value

    early = block.shape[0]
    copies = fetch(jac_ref, jac_ref.shape[0] - early, block, sems)
    copies.append(pltpu.make_async_copy(weight_ref, weights, small_sems.at[0]))
    copies.append(pltpu.make_async_copy(scale_ref, scales, small_sems.at[1]))
    copies[-2].start()
    copies[-1].start()
    for copy in copies:
        copy.wait()
    groups = early // BLOCK
    weight_t = weights[...].T[:, weights.shape[0] - groups :]
    scale_rows(block, weight_t, groups, scales[...], write)


def early_rows(jacobian, weight, scale, early):
    width = jacobian.shape[1]
    return pl.pallas_call(
        early_kernel,
        out_shape=shaped(early, width),
        in_specs=[HBM, HBM, HBM],
        out_specs=VMEM,
        scratch_shapes=[
            pltpu.VMEM((early, width), jnp.float32),
            pltpu.VMEM(weight.shape, jnp.float32),
            pltpu.VMEM(scale.shape, jnp.float32),
            pltpu.SemaphoreType.DMA((chunks(early),)),
            pltpu.SemaphoreType.DMA((2,)),
        ],
        compiler_params=limit(58),
        cost_estimate=cost(early * width, 8 * early * width),
        name="early_rows",
    )(jacobian, weight, scale)


def rows_of(scaled, start, rows):
    def body(x_ref, out_ref):
        out_ref[...] = x_ref[pl.ds(start, rows), :]

    return pl.pallas_call(
        body,
        out_shape=shaped(rows, scaled.shape[1]),
        in_specs=[VMEM],
        out_specs=VMEM,
        compiler_params=limit(8),
        cost_estimate=cost(1, 1),
        name="rows_of",
    )(scaled)


def gram_kernel(jac_ref, weight_ref, scale_ref, out_ref, keep_ref, send_ref, parts, total):
    step = pl.program_id(0)
    width = jac_ref.shape[1]
    weight_t = weight_ref[...].T

    def write(rows, value):
        out_ref[rows, :] = value
        high, rest = split(value)
        parts[rows, :width] = high
        parts[rows, width:] = rest

    scale_rows(jac_ref, weight_t, jac_ref.shape[0] // BLOCK, scale_ref[...], write)
    product = dot(parts[:, :width], parts[...], ((0,), (0,)))

    @pl.when(step == 0)
    def _():
        total[...] = product

    @pl.when(step > 0)
    def _():
        total[...] += product

    @pl.when(step == pl.num_programs(0) - 1)
    def _():
        cross = total[:, width:]
        gram = total[:, :width] + (cross + cross.T)
        size = BLOCK
        half = size // 2
        first = gram[:size, :size]
        middle = gram[:size, size:]
        second = gram[size:, size:]
        odd = lax.axis_index("rows") % 2 == 1
        low_top, low_end = first, middle[:half]
        high_top, high_end = middle[half:], second
        low = jnp.concatenate([low_top, low_end], 0)
        high = jnp.concatenate([high_top, high_end], 0)
        keep_ref[...] = jnp.where(odd, high, low)
        send_ref[...] = jnp.where(odd, low, high)


def gram_of(jacobian, weight, scale):
    rows, width = jacobian.shape
    chunk = 1024
    half = 3 * BLOCK // 2
    return pl.pallas_call(
        gram_kernel,
        grid=(rows // chunk,),
        out_shape=(shaped(rows, width), shaped(half, BLOCK), shaped(half, BLOCK)),
        in_specs=[
            pl.BlockSpec((chunk, width), lambda i: (i, 0)),
            pl.BlockSpec((chunk // BLOCK, BLOCK), lambda i: (i, 0)),
            pl.BlockSpec((1, width), lambda i: (0, 0)),
        ],
        out_specs=(
            pl.BlockSpec((chunk, width), lambda i: (i, 0)),
            pl.BlockSpec((half, BLOCK), lambda i: (0, 0)),
            pl.BlockSpec((half, BLOCK), lambda i: (0, 0)),
        ),
        scratch_shapes=[
            pltpu.VMEM((chunk, 2 * width), jnp.bfloat16),
            pltpu.VMEM((width, 2 * width), jnp.float32),
        ],
        compiler_params=limit(20),
        cost_estimate=cost(4 * rows * width * width, 8 * rows * width),
        name="scaled_gram",
    )(jacobian, weight, scale)


def sum_pieces(keep, send, axis):
    own = keep + swap(send, axis, 1)
    bit = 2
    while bit < lax.axis_size(axis):
        own = own + swap(own, axis, bit)
        bit *= 2
    return own, swap(own, axis, 1)


def run_rounds(count, turn_ref, after_ref, diag_ref):
    size = BLOCK
    eye = lax.broadcasted_iota(jnp.int32, (size, size), 0) == lax.broadcasted_iota(
        jnp.int32, (size, size), 1
    )
    rows = lax.broadcasted_iota(jnp.int32, (2 * size, 2 * size), 0)
    cols = lax.broadcasted_iota(jnp.int32, (2 * size, 2 * size), 1)
    turn_ref[...] = jnp.where(rows == cols, 1.0, 0.0).astype(jnp.float32)

    def diagonal(block):
        row = jnp.sum(jnp.where(eye, block, 0.0), axis=0, keepdims=True)
        return jnp.broadcast_to(row, (8, size))

    def tall(row_tile, height):
        return jnp.concatenate([row_tile] * (height // 8), 0)

    def column(square):
        return jnp.sum(jnp.where(eye, square, 0.0), axis=1, keepdims=True)

    up, low = pl.ds(0, size), pl.ds(size, size)

    def one_round(index, carry):
        first, second = diag_ref[0], diag_ref[1]
        a_blk, c_blk = after_ref[up, up], after_ref[up, low]
        l_blk, d_blk = after_ref[low, up], after_ref[low, low]
        cross = diagonal(c_blk)
        diff = second - first
        radius = jnp.sqrt(diff * diff + 4.0 * cross * cross)
        signs = jnp.where(diff >= 0.0, 1.0, -1.0)
        tangent = signs * 2.0 * cross / (jnp.abs(diff) + radius)
        cos_t = 1.0 / jnp.sqrt(1.0 + tangent * tangent)
        sin_t = cos_t * tangent
        cos_r, sin_r = tall(cos_t, size), tall(sin_t, size)
        cos_c, sin_c = column(cos_r), column(sin_r)

        a_row = cos_c * a_blk - sin_c * l_blk
        c_row = cos_c * c_blk - sin_c * d_blk
        l_row = sin_c * a_blk + cos_c * l_blk
        d_row = sin_c * c_blk + cos_c * d_blk
        after_ref[up, up] = cos_r * a_row - sin_r * c_row
        after_ref[up, low] = pltpu.roll(sin_r * a_row + cos_r * c_row, size - 1, 1)
        after_ref[low, up] = pltpu.roll(cos_r * l_row - sin_r * d_row, size - 1, 0)
        after_ref[low, low] = pltpu.roll(
            pltpu.roll(sin_r * l_row + cos_r * d_row, size - 1, 0), size - 1, 1
        )
        cos_q, sin_q = tall(cos_t, 2 * size), tall(sin_t, 2 * size)
        q_up, q_low = turn_ref[:, up], turn_ref[:, low]
        turn_ref[:, up] = cos_q * q_up - sin_q * q_low
        turn_ref[:, low] = pltpu.roll(sin_q * q_up + cos_q * q_low, size - 1, 1)
        shift = tangent * cross
        diag_ref[0] = first - shift
        diag_ref[1] = pltpu.roll(second + shift, size - 1, 1)
        return carry

    diag_ref[0] = diagonal(after_ref[up, up])
    diag_ref[1] = diagonal(after_ref[low, low])
    lax.fori_loop(0, count, one_round, 0)


def first_kernel(
    count_ref, flag_ref, own_ref, other_ref,
    stay_ref, travel_ref, piece_ref, gram_ref, wstay_ref, wtravel_ref,
    turn_ref, after_ref, diag_ref, pack_ref,
):
    size = BLOCK
    half = size // 2
    device = lax.axis_index("rows")
    odd = device % 2 == 1
    own, other = own_ref[...], other_ref[...]
    low, high = jnp.where(odd, other, own), jnp.where(odd, own, other)
    middle = jnp.concatenate([low[size:], high[:half]], 0)
    after_ref[:size, :size] = low[:size]
    after_ref[:size, size:] = middle
    after_ref[size:, :size] = middle.T
    after_ref[size:, size:] = high[half:]
    run_rounds(count_ref[0], turn_ref, after_ref, diag_ref)

    moves_left = flag_ref[0] == 1
    left, right = turn_ref[:, :size], turn_ref[:, size:]
    travel, stay = jnp.where(moves_left, left, right), jnp.where(moves_left, right, left)
    stay_ref[...] = stay
    travel_ref[...] = travel
    first, second = after_ref[:size, :size], after_ref[size:, size:]
    gram_ref[...] = jnp.where(moves_left, second, first)
    pack_ref[: 2 * size] = travel
    pack_ref[2 * size : 4 * size] = stay
    pack_ref[4 * size :] = jnp.where(moves_left, first, second)
    share = piece_ref.shape[0]
    place = (device % 2) * 2 + device // 2 % 2
    piece_ref[...] = pack_ref[pl.ds(pl.multiple_of(place * share, 8), share), :]

    height = wstay_ref.shape[0]
    start = device * height
    here = start // (2 * size) == lax.axis_index("blk")
    offset = pl.multiple_of(start % (2 * size), height)
    rows = pl.ds(offset, height)
    wstay_ref[...] = jnp.where(here, stay_ref[rows, :], 0.0)
    wtravel_ref[...] = jnp.where(here, travel_ref[rows, :], 0.0)


def first_rounds(count, flag, own, other, basis_rows):
    size = BLOCK
    share = 5 * size // 4
    return pl.pallas_call(
        first_kernel,
        out_shape=(
            shaped(2 * size, size),
            shaped(2 * size, size),
            shaped(share, size),
            shaped(size, size),
            shaped(basis_rows, size),
            shaped(basis_rows, size),
        ),
        in_specs=[SMEM, SMEM, VMEM, VMEM],
        out_specs=(VMEM,) * 6,
        scratch_shapes=[
            pltpu.VMEM((2 * size, 2 * size), jnp.float32),
            pltpu.VMEM((2 * size, 2 * size), jnp.float32),
            pltpu.VMEM((2, 8, size), jnp.float32),
            pltpu.VMEM((5 * size, size), jnp.float32),
        ],
        compiler_params=limit(8),
        cost_estimate=cost(4e9, 1e6),
        name="first_rounds",
    )(count, flag, own, other)


def second_kernel(
    count_ref, flag_ref, own_ref, other_ref, gram_ref, near_ref,
    stay_ref, travel_ref, turn_ref, after_ref, diag_ref,
):
    size = BLOCK
    odd = lax.axis_index("rows") % 2 == 1
    own, other = own_ref[...], other_ref[...]
    middle = jnp.concatenate([jnp.where(odd, other, own), jnp.where(odd, own, other)], 0)
    after_ref[:size, :size] = gram_ref[...]
    after_ref[:size, size:] = middle
    after_ref[size:, :size] = middle.T
    after_ref[size:, size:] = near_ref[...]
    run_rounds(count_ref[1], turn_ref, after_ref, diag_ref)

    moves_left = flag_ref[1] == 1
    left, right = turn_ref[:, :size], turn_ref[:, size:]
    travel_ref[...] = jnp.where(moves_left, left, right)
    stay_ref[...] = jnp.where(moves_left, right, left)


def second_rounds(count, flag, own, other, gram, near):
    size = BLOCK
    return pl.pallas_call(
        second_kernel,
        out_shape=(shaped(2 * size, size), shaped(2 * size, size)),
        in_specs=[SMEM, SMEM] + [VMEM] * 4,
        out_specs=(VMEM,) * 2,
        scratch_shapes=[
            pltpu.VMEM((2 * size, 2 * size), jnp.float32),
            pltpu.VMEM((2 * size, 2 * size), jnp.float32),
            pltpu.VMEM((2, 8, size), jnp.float32),
        ],
        compiler_params=limit(8),
        cost_estimate=cost(4e9, 1e6),
        name="second_rounds",
    )(count, flag, own, other, gram, near)


def tiles(total):
    done = 0
    while done < total:
        size = min(TILE, total - done)
        yield pl.ds(done, size), done, size
        done += size


def product_kernel(start, head, x_ref, turn_ref, head_ref, out_ref):
    turn = paired(turn_ref[: x_ref.shape[1], :])
    if head:
        out_ref[:head, :] = head_ref[...]
    for _, done, size in tiles(out_ref.shape[0] - head):
        rows = x_ref[pl.ds(start + done, size), :]
        out_ref[pl.ds(head + done, size), :] = times(rows, turn)


def product(scaled, turn, top, start, rows, name):
    head = 0 if top is None else top.shape[0]
    top = turn if top is None else top

    def body(*refs):
        product_kernel(start, head, *refs)

    return pl.pallas_call(
        body,
        out_shape=shaped(head + rows, BLOCK),
        in_specs=[VMEM] * 3,
        out_specs=VMEM,
        compiler_params=limit(16),
        cost_estimate=cost(6 * rows * 256 * 128, 1536 * rows),
        name=name,
    )(scaled, turn, top)


def stay_rows(scaled, turn, top, pieces):
    head, rows = top.shape[0], scaled.shape[0]

    def body(x_ref, turn_ref, head_ref, out_ref, *piece_refs):
        product_kernel(0, head, x_ref, turn_ref, head_ref, out_ref)
        at = 0
        for piece in piece_refs:
            piece[...] = out_ref[pl.ds(at, piece.shape[0]), :]
            at += piece.shape[0]

    outs = (shaped(head + rows, BLOCK),) + tuple(shaped(piece, BLOCK) for piece in pieces)
    return pl.pallas_call(
        body,
        out_shape=outs,
        in_specs=[VMEM] * 3,
        out_specs=(VMEM,) * len(outs),
        compiler_params=limit(16),
        cost_estimate=cost(6 * rows * 256 * 128, 1536 * rows),
        name="stay_rows",
    )(scaled, turn, top)


def cross_of(left_ref, right_ref, left_at, right_at, rows):
    total = None
    for _, done, size in tiles(rows):
        left = split(left_ref[pl.ds(left_at + done, size), :])
        right = split(right_ref[pl.ds(right_at + done, size), :])
        part = dot_parts(left, right, ((0,), (0,)))
        total = part if total is None else total + part
    return total


def joined(first, second):
    rows = first.shape[0]

    def body(first_ref, second_ref, out_ref):
        out_ref[:rows, :] = first_ref[...]
        out_ref[rows:, :] = second_ref[...]

    return pl.pallas_call(
        body,
        out_shape=shaped(2 * rows, first.shape[1]),
        in_specs=[VMEM] * 2,
        out_specs=VMEM,
        compiler_params=limit(4),
        cost_estimate=cost(1, 1),
        name="joined",
    )(first, second)


def gathered(piece, axis):
    both = joined(piece, swap(piece, axis, 2))
    return both, swap(both, axis, 1)


def near_rows(stay, one, two, pieces):
    rows = one.shape[0] + two.shape[0]
    share = pieces[0].shape[0] // 2

    def body(*refs):
        stay_ref, one_ref, two_ref, own_ref, other_ref = refs[:5]
        travel_ref, near_ref, gram_ref, cross_ref, pack = refs[5:]
        device = lax.axis_index("rows")
        core, parity = device % 2, device // 2 % 2
        for side, piece in ((core, own_ref), (1 - core, other_ref)):
            for part, place in ((0, parity), (1, 1 - parity)):
                at = pl.multiple_of((side * 2 + place) * share, 8)
                pack[pl.ds(at, share), :] = piece[pl.ds(part * share, share), :]
        size = BLOCK
        turns = split(jnp.concatenate([pack[: 2 * size], pack[2 * size : 4 * size]], 1))
        gram_ref[...] = pack[4 * size :]
        at = 0
        for early_ref in (one_ref, two_ref):
            for part, done, length in tiles(early_ref.shape[0]):
                both = dot_parts(split(early_ref[part, :]), turns)
                travel_ref[pl.ds(at + done, length), :] = both[:, :size]
                near_ref[pl.ds(at + done, length), :] = both[:, size:]
            at += early_ref.shape[0]
        cross_ref[...] = cross_of(stay_ref, travel_ref, stay_ref.shape[0] - at, 0, at)

    return pl.pallas_call(
        body,
        out_shape=(
            shaped(rows, BLOCK),
            shaped(rows, BLOCK),
            shaped(BLOCK, BLOCK),
            shaped(BLOCK, BLOCK),
        ),
        in_specs=[VMEM] * 5,
        out_specs=(VMEM,) * 4,
        scratch_shapes=[pltpu.VMEM((5 * BLOCK, BLOCK), jnp.float32)],
        compiler_params=limit(16),
        cost_estimate=cost(15 * rows * 256 * 128, 2560 * rows),
        name="near_rows",
    )(stay, one, two, *pieces)


def add_cross(stay, arrived, before, stay_at, arrived_at, last):
    rows = arrived.shape[0] - arrived_at
    half = BLOCK // 2

    def body(stay_ref, arrived_ref, before_ref, *out_refs):
        cross = before_ref[...] + cross_of(stay_ref, arrived_ref, stay_at, arrived_at, rows)
        if last:
            odd = lax.axis_index("rows") % 2 == 1
            out_refs[0][...] = jnp.where(odd, cross[half:], cross[:half])
            out_refs[1][...] = jnp.where(odd, cross[:half], cross[half:])
        else:
            out_refs[0][...] = cross

    out_shape = (shaped(half, BLOCK),) * 2 if last else (shaped(BLOCK, BLOCK),)
    return pl.pallas_call(
        body,
        out_shape=out_shape,
        in_specs=[VMEM] * 3,
        out_specs=(VMEM,) * len(out_shape),
        compiler_params=limit(16),
        cost_estimate=cost(3 * rows * 256 * 128, 1024 * rows),
        name="last_cross" if last else "add_cross",
    )(stay, arrived, before)


def mixed(stay_ref, arrived_ref, turn, stay_at, arrived_at, size):
    both = jnp.concatenate(
        [stay_ref[pl.ds(stay_at, size), :], arrived_ref[pl.ds(arrived_at, size), :]], 1
    )
    return times(both, turn)


def staying(stay, arrived, turn):
    rows = stay.shape[0]

    def body(*refs):
        stay_ref, *arrived_refs, turn_ref, out_ref = refs
        parts = paired(turn_ref[...])
        at = 0
        for arrived_ref in arrived_refs:
            for _, done, size in tiles(arrived_ref.shape[0]):
                out_ref[pl.ds(at + done, size), :] = mixed(
                    stay_ref, arrived_ref, parts, at + done, done, size
                )
            at += arrived_ref.shape[0]

    return pl.pallas_call(
        body,
        out_shape=shaped(rows, BLOCK),
        in_specs=[VMEM] * (2 + len(arrived)),
        out_specs=VMEM,
        compiler_params=limit(20),
        cost_estimate=cost(6 * rows * 256 * 128, 1536 * rows),
        name="staying",
    )(stay, *arrived, turn)


def covering(pieces, start, size):
    at = 0
    for index, rows in enumerate(pieces):
        begin, end = max(start, at), min(start + size, at + rows)
        if begin < end:
            yield index, begin - at, end - begin
        at += rows


def arriving(left, head, stays, travels, turn):
    total = left.shape[0]
    count = len(stays)
    stay_rows_in = [stay.shape[0] for stay in stays]
    flat, places, travel_rows_in = [], [], []
    for travel in travels:
        parts = travel if isinstance(travel, tuple) else (travel,)
        places.append((len(flat), len(parts)))
        travel_rows_in.append(parts[0].shape[0])
        flat.extend(parts)
    blocks = []
    at = 0
    while at < total:
        size = min(TILE, total - at, (head if at < head else total) - at)
        blocks.append((at, size))
        at += size

    def body(*refs):
        left_ref, turn_ref, *rest = refs
        stay_refs, travel_refs = rest[:count], rest[count : count + len(flat)]
        out_ref, basis_ref, whole, sems = rest[count + len(flat) :]
        odd_pair = lax.axis_index("blk") % 2 == 1
        turn = paired(turn_ref[...])

        def travel_part(index, first, rows):
            place, ways = places[index]
            part = travel_refs[place][pl.ds(first, rows), :]
            if ways == 2:
                part = jnp.where(odd_pair, part, travel_refs[place + 1][pl.ds(first, rows), :])
            return part

        copies = []
        for number, (at, size) in enumerate(blocks):
            stay = [
                stay_refs[index][pl.ds(first, rows), :]
                for index, first, rows in covering(stay_rows_in, at, size)
            ]
            travel = [
                travel_part(index, first, rows)
                for index, first, rows in covering(travel_rows_in, at, size)
            ]
            both = jnp.concatenate([jnp.concatenate(stay, 0), jnp.concatenate(travel, 0)], 1)
            right = times(both, turn)
            span = pl.ds(at, size)
            if at < head:
                basis_ref[span, :BLOCK] = left_ref[span, :]
                basis_ref[span, BLOCK:] = right
                continue
            whole[span, :BLOCK] = left_ref[span, :]
            whole[span, BLOCK:] = right
            copy = pltpu.make_async_copy(
                whole.at[span, :], out_ref.at[pl.ds(at - head, size), :], sems.at[number]
            )
            copy.start()
            copies.append(copy)
        for copy in copies:
            copy.wait()

    return pl.pallas_call(
        body,
        out_shape=(shaped(total - head, 2 * BLOCK), shaped(head, 2 * BLOCK)),
        in_specs=[VMEM] * (2 + count + len(flat)),
        out_specs=(HBM, VMEM),
        scratch_shapes=[
            pltpu.VMEM((total, 2 * BLOCK), jnp.float32),
            pltpu.SemaphoreType.DMA((len(blocks),)),
        ],
        compiler_params=limit(20),
        cost_estimate=cost(6 * total * 256 * 128, 2048 * total),
        name="arriving",
    )(left, turn, *stays, *flat)


def per_device(jacobian, row_weight, col_scale, round_count, move_flag):
    rows, width = jacobian.shape
    move_flag = move_flag.reshape(STEPS)
    weight = row_weight.reshape(rows // BLOCK, BLOCK)
    scale = col_scale.reshape(1, width)
    head = width * lax.axis_size("blk") // lax.axis_size("rows")
    early_count = EARLY + EARLY_MORE
    late = rows - early_count
    cut = (late - head) // 2 // BLOCK * BLOCK
    starts = (0, cut, late)
    sizes = (head + cut, late - cut)
    stay_sizes = (sizes[0] - BLOCK, sizes[1] + BLOCK)
    barrier = lax.optimization_barrier

    early, jacobian = lax.optimization_barrier(
        (early_rows(jacobian, weight, scale, EARLY), jacobian)
    )
    early_near = from_behind(early, "blk", 1)
    scaled, keep, send = gram_of(jacobian, weight, scale)
    more_near = from_behind(rows_of(scaled, late, EARLY_MORE), "blk", 1)
    own, other = sum_pieces(keep, send, "rows")
    own, early_near = barrier((own, early_near))
    stay_turn, travel_turn, piece, gram, w_stay, w_travel = first_rounds(
        round_count, move_flag, own, other, head
    )
    piece = from_behind(piece, "blk", 1)

    go = [
        product(scaled, travel_turn, w_travel, 0, cut, "travel_0"),
        product(scaled, travel_turn, None, cut, late - cut, "travel_1"),
    ]
    go_early = product(scaled, travel_turn, None, late, early_count, "travel_early")
    stay, *stays = stay_rows(scaled, stay_turn, w_stay, stay_sizes)

    near, stays_near = [None] * 2, [None] * 2
    first_odd = hop(go[0], "blk", 1)
    passing, piece, more_near = barrier(
        (passed_on(go[0], first_odd, "pass_0"), piece, more_near)
    )
    near[0] = swap(passing, "blk", 1)
    go[1], first_odd, stay, stays[0], go_early = barrier(
        (go[1], first_odd, stay, stays[0], go_early)
    )
    second = from_behind(go[1], "blk", 2)
    passing, near[0] = barrier((passed_on(go[1], second, "pass_1"), near[0]))
    near[1] = swap(passing, "blk", 1)

    near_early, stay_early, gram_near, cross = near_rows(
        stay, more_near, early_near, gathered(piece, "rows")
    )
    stays[0], cross = barrier((stays[0], cross))
    stay_odd = hop(stays[0], "blk", 1)
    go[0], second = barrier((go[0], second))
    first_even = hop(go[0], "blk", 0)
    passing, near[1] = barrier((passed_on(stays[0], stay_odd, "pass_2"), near[1]))
    stays_near[0] = swap(passing, "blk", 1)
    stays[1], stay_odd = barrier((stays[1], stay_odd))
    stay_odd_two = hop(stays[1], "blk", 1)

    (cross,) = add_cross(stay, near[0], cross, head, head, False)
    keep, send = add_cross(stay, near[1], cross, sizes[0], 0, True)
    keep, send, first_even, go_early = barrier((keep, send, first_even, go_early))
    early_two = from_behind(go_early, "blk", 2)
    own, other = sum_pieces(keep, send, "rows")
    own, stays_near[0] = barrier((own, stays_near[0]))
    stays[1], stay_odd_two, own = barrier((stays[1], stay_odd_two, own))
    stays_near[1] = swap(passed_on(stays[1], stay_odd_two, "pass_3"), "blk", 1)
    stay_next, travel_next = second_rounds(round_count, move_flag, own, other, gram, gram_near)
    turn_near = from_behind(travel_next, "blk", 1)
    left = staying(stay, near + [near_early], stay_next)
    left, early_two = barrier((left, early_two))
    travels = [(first_odd, first_even), second, early_two]
    stays_near.append(stay_early)
    return arriving(left, head, stays_near, travels, turn_near)


def solution(mesh):
    in_specs = (P("rows", "blk"), P("rows"), P("blk"), P(), P(None, "blk"))
    out_specs = (P("rows", "blk"), P("rows", "blk"))
    return jax.shard_map(
        per_device, mesh=mesh, in_specs=in_specs, out_specs=out_specs, check_vma=False
    )
```

```python
import jax
import jax.numpy as jnp
from jax import lax
from jax.experimental import pallas as pl
from jax.experimental.pallas import tpu as pltpu
from jax.sharding import PartitionSpec as P

BLOCK = 128
STEPS = 2
TILE = 256
EARLY = 768
EARLY_MORE = 1152
CHUNK = 512
MIB = 1024 * 1024

VMEM = pl.BlockSpec(memory_space=pltpu.VMEM)
SMEM = pl.BlockSpec(memory_space=pltpu.SMEM)
ANY = pl.BlockSpec(memory_space=pl.ANY)
HBM = pl.BlockSpec(memory_space=pltpu.HBM)


def shaped(*dims):
    return jax.ShapeDtypeStruct(dims, jnp.float32)


def limit(mib):
    return pltpu.CompilerParams(vmem_limit_bytes=mib * MIB)


def cost(flops, moved):
    return pl.CostEstimate(flops=1000, bytes_accessed=1000, transcendentals=0)


def from_behind(block, axis, distance):
    devices = range(lax.axis_size(axis))
    route = [((i - distance) % len(devices), i) for i in devices]
    return lax.ppermute(block, axis, route)


def swap(block, axis, bit):
    return lax.ppermute(block, axis, [(i, i ^ bit) for i in range(lax.axis_size(axis))])


def hop(block, axis, parity):
    size = lax.axis_size(axis)
    return lax.ppermute(block, axis, [(i, (i + 2) % size) for i in range(parity, size, 2)])


def passed_on(block, behind, name):
    def body(block_ref, behind_ref, out_ref):
        odd = lax.axis_index("blk") % 2 == 1

        @pl.when(odd)
        def _():
            out_ref[...] = behind_ref[...]

        @pl.when(jnp.logical_not(odd))
        def _():
            out_ref[...] = block_ref[...]

    return pl.pallas_call(
        body,
        out_shape=shaped(*block.shape),
        in_specs=[VMEM] * 2,
        out_specs=VMEM,
        compiler_params=limit(8),
        cost_estimate=cost(1, 1),
        name=name,
    )(block, behind)


def split(value):
    high = value.astype(jnp.bfloat16)
    rest = (value - high.astype(jnp.float32)).astype(jnp.bfloat16)
    return high, rest


def dot(left, right, dims=((1,), (0,))):
    return lax.dot_general(left, right, (dims, ((), ())), preferred_element_type=jnp.float32)


def dot_parts(left, right, dims=((1,), (0,))):
    l_high, l_rest = left
    r_high, r_rest = right
    small = dot(l_high, r_rest, dims) + dot(l_rest, r_high, dims)
    return dot(l_high, r_high, dims) + small


def paired(small):
    high, rest = split(small)
    return jnp.concatenate([high, rest], 1), high


def times(value, pair):
    both, first = pair
    width = first.shape[1]
    high, rest = split(value)
    wide = dot(high, both)
    return wide[:, :width] + (wide[:, width:] + dot(rest, first))


def scale_rows(source, weight_t, groups, col_scale, write):
    for group in range(groups):
        rows = pl.ds(group * BLOCK, BLOCK)
        write(rows, source[rows, :] * weight_t[:, group : group + 1] * col_scale)


def fetch(source, start, block, sems):
    copies = []
    for done in range(0, block.shape[0], CHUNK):
        size = min(CHUNK, block.shape[0] - done)
        copies.append(
            pltpu.make_async_copy(
                source.at[pl.ds(start + done, size), :],
                block.at[pl.ds(done, size), :],
                sems.at[len(copies)],
            )
        )
    for copy in copies:
        copy.start()
    return copies


def chunks(rows):
    return -(-rows // CHUNK)


def early_kernel(jac_ref, weight_ref, scale_ref, out_ref, block, weights, scales, sems, small_sems):
    def write(rows, value):
        out_ref[rows, :] = value

    early = block.shape[0]
    copies = fetch(jac_ref, jac_ref.shape[0] - early, block, sems)
    copies.append(pltpu.make_async_copy(weight_ref, weights, small_sems.at[0]))
    copies.append(pltpu.make_async_copy(scale_ref, scales, small_sems.at[1]))
    copies[-2].start()
    copies[-1].start()
    for copy in copies:
        copy.wait()
    groups = early // BLOCK
    weight_t = weights[...].T[:, weights.shape[0] - groups :]
    scale_rows(block, weight_t, groups, scales[...], write)


def early_rows(jacobian, weight, scale, early):
    width = jacobian.shape[1]
    return pl.pallas_call(
        early_kernel,
        out_shape=shaped(early, width),
        in_specs=[HBM, HBM, HBM],
        out_specs=VMEM,
        scratch_shapes=[
            pltpu.VMEM((early, width), jnp.float32),
            pltpu.VMEM(weight.shape, jnp.float32),
            pltpu.VMEM(scale.shape, jnp.float32),
            pltpu.SemaphoreType.DMA((chunks(early),)),
            pltpu.SemaphoreType.DMA((2,)),
        ],
        compiler_params=limit(58),
        cost_estimate=cost(early * width, 8 * early * width),
        name="early_rows",
    )(jacobian, weight, scale)


def rows_of(scaled, start, rows):
    def body(x_ref, out_ref):
        out_ref[...] = x_ref[pl.ds(start, rows), :]

    return pl.pallas_call(
        body,
        out_shape=shaped(rows, scaled.shape[1]),
        in_specs=[VMEM],
        out_specs=VMEM,
        compiler_params=limit(8),
        cost_estimate=cost(1, 1),
        name="rows_of",
    )(scaled)


def gram_kernel(jac_ref, weight_ref, scale_ref, out_ref, keep_ref, send_ref, parts, total):
    step = pl.program_id(0)
    width = jac_ref.shape[1]
    weight_t = weight_ref[...].T

    def write(rows, value):
        out_ref[rows, :] = value
        high, rest = split(value)
        parts[rows, :width] = high
        parts[rows, width:] = rest

    scale_rows(jac_ref, weight_t, jac_ref.shape[0] // BLOCK, scale_ref[...], write)
    product = dot(parts[:, :width], parts[...], ((0,), (0,)))

    @pl.when(step == 0)
    def _():
        total[...] = product

    @pl.when(step > 0)
    def _():
        total[...] += product

    @pl.when(step == pl.num_programs(0) - 1)
    def _():
        cross = total[:, width:]
        gram = total[:, :width] + (cross + cross.T)
        size = BLOCK
        half = size // 2
        first = gram[:size, :size]
        middle = gram[:size, size:]
        second = gram[size:, size:]
        odd = lax.axis_index("rows") % 2 == 1
        low_top, low_end = first, middle[:half]
        high_top, high_end = middle[half:], second
        low = jnp.concatenate([low_top, low_end], 0)
        high = jnp.concatenate([high_top, high_end], 0)
        keep_ref[...] = jnp.where(odd, high, low)
        send_ref[...] = jnp.where(odd, low, high)


def gram_of(jacobian, weight, scale):
    rows, width = jacobian.shape
    chunk = 1024
    half = 3 * BLOCK // 2
    return pl.pallas_call(
        gram_kernel,
        grid=(rows // chunk,),
        out_shape=(shaped(rows, width), shaped(half, BLOCK), shaped(half, BLOCK)),
        in_specs=[
            pl.BlockSpec((chunk, width), lambda i: (i, 0)),
            pl.BlockSpec((chunk // BLOCK, BLOCK), lambda i: (i, 0)),
            pl.BlockSpec((1, width), lambda i: (0, 0)),
        ],
        out_specs=(
            pl.BlockSpec((chunk, width), lambda i: (i, 0)),
            pl.BlockSpec((half, BLOCK), lambda i: (0, 0)),
            pl.BlockSpec((half, BLOCK), lambda i: (0, 0)),
        ),
        scratch_shapes=[
            pltpu.VMEM((chunk, 2 * width), jnp.bfloat16),
            pltpu.VMEM((width, 2 * width), jnp.float32),
        ],
        compiler_params=limit(20),
        cost_estimate=cost(4 * rows * width * width, 8 * rows * width),
        name="scaled_gram",
    )(jacobian, weight, scale)


def sum_pieces(keep, send, axis):
    own = keep + swap(send, axis, 1)
    bit = 2
    while bit < lax.axis_size(axis):
        own = own + swap(own, axis, bit)
        bit *= 2
    return own, swap(own, axis, 1)


def run_rounds(count, turn_ref, after_ref, diag_ref):
    size = BLOCK
    eye = lax.broadcasted_iota(jnp.int32, (size, size), 0) == lax.broadcasted_iota(
        jnp.int32, (size, size), 1
    )
    rows = lax.broadcasted_iota(jnp.int32, (2 * size, 2 * size), 0)
    cols = lax.broadcasted_iota(jnp.int32, (2 * size, 2 * size), 1)
    turn_ref[...] = jnp.where(rows == cols, 1.0, 0.0).astype(jnp.float32)

    def diagonal(block):
        row = jnp.sum(jnp.where(eye, block, 0.0), axis=0, keepdims=True)
        return jnp.broadcast_to(row, (8, size))

    def tall(row_tile, height):
        return jnp.concatenate([row_tile] * (height // 8), 0)

    def column(square):
        return jnp.sum(jnp.where(eye, square, 0.0), axis=1, keepdims=True)

    up, low = pl.ds(0, size), pl.ds(size, size)

    def one_round(index, carry):
        first, second = diag_ref[0], diag_ref[1]
        a_blk, c_blk = after_ref[up, up], after_ref[up, low]
        l_blk, d_blk = after_ref[low, up], after_ref[low, low]
        cross = diagonal(c_blk)
        diff = second - first
        radius = jnp.sqrt(diff * diff + 4.0 * cross * cross)
        signs = jnp.where(diff >= 0.0, 1.0, -1.0)
        tangent = signs * 2.0 * cross / (jnp.abs(diff) + radius)
        cos_t = 1.0 / jnp.sqrt(1.0 + tangent * tangent)
        sin_t = cos_t * tangent
        cos_r, sin_r = tall(cos_t, size), tall(sin_t, size)
        cos_c, sin_c = column(cos_r), column(sin_r)

        a_row = cos_c * a_blk - sin_c * l_blk
        c_row = cos_c * c_blk - sin_c * d_blk
        l_row = sin_c * a_blk + cos_c * l_blk
        d_row = sin_c * c_blk + cos_c * d_blk
        after_ref[up, up] = cos_r * a_row - sin_r * c_row
        after_ref[up, low] = pltpu.roll(sin_r * a_row + cos_r * c_row, size - 1, 1)
        after_ref[low, up] = pltpu.roll(cos_r * l_row - sin_r * d_row, size - 1, 0)
        after_ref[low, low] = pltpu.roll(
            pltpu.roll(sin_r * l_row + cos_r * d_row, size - 1, 0), size - 1, 1
        )
        cos_q, sin_q = tall(cos_t, 2 * size), tall(sin_t, 2 * size)
        q_up, q_low = turn_ref[:, up], turn_ref[:, low]
        turn_ref[:, up] = cos_q * q_up - sin_q * q_low
        turn_ref[:, low] = pltpu.roll(sin_q * q_up + cos_q * q_low, size - 1, 1)
        shift = tangent * cross
        diag_ref[0] = first - shift
        diag_ref[1] = pltpu.roll(second + shift, size - 1, 1)
        return carry

    diag_ref[0] = diagonal(after_ref[up, up])
    diag_ref[1] = diagonal(after_ref[low, low])
    lax.fori_loop(0, count, one_round, 0)


def first_kernel(
    count_ref, flag_ref, own_ref, other_ref,
    stay_ref, travel_ref, piece_ref, gram_ref, wstay_ref, wtravel_ref,
    turn_ref, after_ref, diag_ref, pack_ref,
):
    size = BLOCK
    half = size // 2
    device = lax.axis_index("rows")
    odd = device % 2 == 1
    own, other = own_ref[...], other_ref[...]
    low, high = jnp.where(odd, other, own), jnp.where(odd, own, other)
    middle = jnp.concatenate([low[size:], high[:half]], 0)
    after_ref[:size, :size] = low[:size]
    after_ref[:size, size:] = middle
    after_ref[size:, :size] = middle.T
    after_ref[size:, size:] = high[half:]
    run_rounds(count_ref[0], turn_ref, after_ref, diag_ref)

    moves_left = flag_ref[0] == 1
    left, right = turn_ref[:, :size], turn_ref[:, size:]
    travel, stay = jnp.where(moves_left, left, right), jnp.where(moves_left, right, left)
    stay_ref[...] = stay
    travel_ref[...] = travel
    first, second = after_ref[:size, :size], after_ref[size:, size:]
    gram_ref[...] = jnp.where(moves_left, second, first)
    pack_ref[: 2 * size] = travel
    pack_ref[2 * size : 4 * size] = stay
    pack_ref[4 * size :] = jnp.where(moves_left, first, second)
    share = piece_ref.shape[0]
    place = (device % 2) * 2 + device // 2 % 2
    piece_ref[...] = pack_ref[pl.ds(pl.multiple_of(place * share, 8), share), :]

    height = wstay_ref.shape[0]
    start = device * height
    here = start // (2 * size) == lax.axis_index("blk")
    offset = pl.multiple_of(start % (2 * size), height)
    rows = pl.ds(offset, height)
    wstay_ref[...] = jnp.where(here, stay_ref[rows, :], 0.0)
    wtravel_ref[...] = jnp.where(here, travel_ref[rows, :], 0.0)


def first_rounds(count, flag, own, other, basis_rows):
    size = BLOCK
    share = 5 * size // 4
    return pl.pallas_call(
        first_kernel,
        out_shape=(
            shaped(2 * size, size),
            shaped(2 * size, size),
            shaped(share, size),
            shaped(size, size),
            shaped(basis_rows, size),
            shaped(basis_rows, size),
        ),
        in_specs=[SMEM, SMEM, VMEM, VMEM],
        out_specs=(VMEM,) * 6,
        scratch_shapes=[
            pltpu.VMEM((2 * size, 2 * size), jnp.float32),
            pltpu.VMEM((2 * size, 2 * size), jnp.float32),
            pltpu.VMEM((2, 8, size), jnp.float32),
            pltpu.VMEM((5 * size, size), jnp.float32),
        ],
        compiler_params=limit(8),
        cost_estimate=cost(4e9, 1e6),
        name="first_rounds",
    )(count, flag, own, other)


def second_kernel(
    count_ref, flag_ref, own_ref, other_ref, gram_ref, near_ref,
    stay_ref, travel_ref, turn_ref, after_ref, diag_ref,
):
    size = BLOCK
    odd = lax.axis_index("rows") % 2 == 1
    own, other = own_ref[...], other_ref[...]
    middle = jnp.concatenate([jnp.where(odd, other, own), jnp.where(odd, own, other)], 0)
    after_ref[:size, :size] = gram_ref[...]
    after_ref[:size, size:] = middle
    after_ref[size:, :size] = middle.T
    after_ref[size:, size:] = near_ref[...]
    run_rounds(count_ref[1], turn_ref, after_ref, diag_ref)

    moves_left = flag_ref[1] == 1
    left, right = turn_ref[:, :size], turn_ref[:, size:]
    travel_ref[...] = jnp.where(moves_left, left, right)
    stay_ref[...] = jnp.where(moves_left, right, left)


def second_rounds(count, flag, own, other, gram, near):
    size = BLOCK
    return pl.pallas_call(
        second_kernel,
        out_shape=(shaped(2 * size, size), shaped(2 * size, size)),
        in_specs=[SMEM, SMEM] + [VMEM] * 4,
        out_specs=(VMEM,) * 2,
        scratch_shapes=[
            pltpu.VMEM((2 * size, 2 * size), jnp.float32),
            pltpu.VMEM((2 * size, 2 * size), jnp.float32),
            pltpu.VMEM((2, 8, size), jnp.float32),
        ],
        compiler_params=limit(8),
        cost_estimate=cost(4e9, 1e6),
        name="second_rounds",
    )(count, flag, own, other, gram, near)


def tiles(total):
    done = 0
    while done < total:
        size = min(TILE, total - done)
        yield pl.ds(done, size), done, size
        done += size


def product_kernel(start, head, x_ref, turn_ref, head_ref, out_ref):
    turn = paired(turn_ref[: x_ref.shape[1], :])
    if head:
        out_ref[:head, :] = head_ref[...]
    for _, done, size in tiles(out_ref.shape[0] - head):
        rows = x_ref[pl.ds(start + done, size), :]
        out_ref[pl.ds(head + done, size), :] = times(rows, turn)


def product(scaled, turn, top, start, rows, name):
    head = 0 if top is None else top.shape[0]
    top = turn if top is None else top

    def body(*refs):
        product_kernel(start, head, *refs)

    return pl.pallas_call(
        body,
        out_shape=shaped(head + rows, BLOCK),
        in_specs=[VMEM] * 3,
        out_specs=VMEM,
        compiler_params=limit(16),
        cost_estimate=cost(6 * rows * 256 * 128, 1536 * rows),
        name=name,
    )(scaled, turn, top)


def stay_rows(scaled, turn, top, pieces):
    head, rows = top.shape[0], scaled.shape[0]

    def body(x_ref, turn_ref, head_ref, out_ref, *piece_refs):
        product_kernel(0, head, x_ref, turn_ref, head_ref, out_ref)
        at = 0
        for piece in piece_refs:
            piece[...] = out_ref[pl.ds(at, piece.shape[0]), :]
            at += piece.shape[0]

    outs = (shaped(head + rows, BLOCK),) + tuple(shaped(piece, BLOCK) for piece in pieces)
    return pl.pallas_call(
        body,
        out_shape=outs,
        in_specs=[VMEM] * 3,
        out_specs=(VMEM,) * len(outs),
        compiler_params=limit(16),
        cost_estimate=cost(6 * rows * 256 * 128, 1536 * rows),
        name="stay_rows",
    )(scaled, turn, top)


def cross_of(left_ref, right_ref, left_at, right_at, rows):
    total = None
    for _, done, size in tiles(rows):
        left = split(left_ref[pl.ds(left_at + done, size), :])
        right = split(right_ref[pl.ds(right_at + done, size), :])
        part = dot_parts(left, right, ((0,), (0,)))
        total = part if total is None else total + part
    return total


def joined(first, second):
    rows = first.shape[0]

    def body(first_ref, second_ref, out_ref):
        out_ref[:rows, :] = first_ref[...]
        out_ref[rows:, :] = second_ref[...]

    return pl.pallas_call(
        body,
        out_shape=shaped(2 * rows, first.shape[1]),
        in_specs=[VMEM] * 2,
        out_specs=VMEM,
        compiler_params=limit(4),
        cost_estimate=cost(1, 1),
        name="joined",
    )(first, second)


def gathered(piece, axis):
    both = joined(piece, swap(piece, axis, 2))
    return both, swap(both, axis, 1)


def near_rows(stay, one, two, pieces):
    rows = one.shape[0] + two.shape[0]
    share = pieces[0].shape[0] // 2

    def body(*refs):
        stay_ref, one_ref, two_ref, own_ref, other_ref = refs[:5]
        travel_ref, near_ref, gram_ref, cross_ref, pack = refs[5:]
        device = lax.axis_index("rows")
        core, parity = device % 2, device // 2 % 2
        for side, piece in ((core, own_ref), (1 - core, other_ref)):
            for part, place in ((0, parity), (1, 1 - parity)):
                at = pl.multiple_of((side * 2 + place) * share, 8)
                pack[pl.ds(at, share), :] = piece[pl.ds(part * share, share), :]
        size = BLOCK
        turns = split(jnp.concatenate([pack[: 2 * size], pack[2 * size : 4 * size]], 1))
        gram_ref[...] = pack[4 * size :]
        at = 0
        for early_ref in (one_ref, two_ref):
            for part, done, length in tiles(early_ref.shape[0]):
                both = dot_parts(split(early_ref[part, :]), turns)
                travel_ref[pl.ds(at + done, length), :] = both[:, :size]
                near_ref[pl.ds(at + done, length), :] = both[:, size:]
            at += early_ref.shape[0]
        cross_ref[...] = cross_of(stay_ref, travel_ref, stay_ref.shape[0] - at, 0, at)

    return pl.pallas_call(
        body,
        out_shape=(
            shaped(rows, BLOCK),
            shaped(rows, BLOCK),
            shaped(BLOCK, BLOCK),
            shaped(BLOCK, BLOCK),
        ),
        in_specs=[VMEM] * 5,
        out_specs=(VMEM,) * 4,
        scratch_shapes=[pltpu.VMEM((5 * BLOCK, BLOCK), jnp.float32)],
        compiler_params=limit(16),
        cost_estimate=cost(15 * rows * 256 * 128, 2560 * rows),
        name="near_rows",
    )(stay, one, two, *pieces)


def add_cross(stay, arrived, before, stay_at, arrived_at, last):
    rows = arrived.shape[0] - arrived_at
    half = BLOCK // 2

    def body(stay_ref, arrived_ref, before_ref, *out_refs):
        cross = before_ref[...] + cross_of(stay_ref, arrived_ref, stay_at, arrived_at, rows)
        if last:
            odd = lax.axis_index("rows") % 2 == 1
            out_refs[0][...] = jnp.where(odd, cross[half:], cross[:half])
            out_refs[1][...] = jnp.where(odd, cross[:half], cross[half:])
        else:
            out_refs[0][...] = cross

    out_shape = (shaped(half, BLOCK),) * 2 if last else (shaped(BLOCK, BLOCK),)
    return pl.pallas_call(
        body,
        out_shape=out_shape,
        in_specs=[VMEM] * 3,
        out_specs=(VMEM,) * len(out_shape),
        compiler_params=limit(16),
        cost_estimate=cost(3 * rows * 256 * 128, 1024 * rows),
        name="last_cross" if last else "add_cross",
    )(stay, arrived, before)


def mixed(stay_ref, arrived_ref, turn, stay_at, arrived_at, size):
    both = jnp.concatenate(
        [stay_ref[pl.ds(stay_at, size), :], arrived_ref[pl.ds(arrived_at, size), :]], 1
    )
    return times(both, turn)


def staying(stay, arrived, turn):
    rows = stay.shape[0]

    def body(*refs):
        stay_ref, *arrived_refs, turn_ref, out_ref = refs
        parts = paired(turn_ref[...])
        at = 0
        for arrived_ref in arrived_refs:
            for _, done, size in tiles(arrived_ref.shape[0]):
                out_ref[pl.ds(at + done, size), :] = mixed(
                    stay_ref, arrived_ref, parts, at + done, done, size
                )
            at += arrived_ref.shape[0]

    return pl.pallas_call(
        body,
        out_shape=shaped(rows, BLOCK),
        in_specs=[VMEM] * (2 + len(arrived)),
        out_specs=VMEM,
        compiler_params=limit(20),
        cost_estimate=cost(6 * rows * 256 * 128, 1536 * rows),
        name="staying",
    )(stay, *arrived, turn)


def covering(pieces, start, size):
    at = 0
    for index, rows in enumerate(pieces):
        begin, end = max(start, at), min(start + size, at + rows)
        if begin < end:
            yield index, begin - at, end - begin
        at += rows


def arriving(left, head, stays, travels, turn):
    total = left.shape[0]
    count = len(stays)
    stay_rows_in = [stay.shape[0] for stay in stays]
    flat, places, travel_rows_in = [], [], []
    for travel in travels:
        parts = travel if isinstance(travel, tuple) else (travel,)
        places.append((len(flat), len(parts)))
        travel_rows_in.append(parts[0].shape[0])
        flat.extend(parts)
    blocks = []
    at = 0
    while at < total:
        size = min(TILE, total - at, (head if at < head else total) - at)
        blocks.append((at, size))
        at += size

    def body(*refs):
        left_ref, turn_ref, *rest = refs
        stay_refs, travel_refs = rest[:count], rest[count : count + len(flat)]
        out_ref, basis_ref, whole, sems = rest[count + len(flat) :]
        odd_pair = lax.axis_index("blk") % 2 == 1
        turn = paired(turn_ref[...])

        def travel_part(index, first, rows):
            place, ways = places[index]
            part = travel_refs[place][pl.ds(first, rows), :]
            if ways == 2:
                part = jnp.where(odd_pair, part, travel_refs[place + 1][pl.ds(first, rows), :])
            return part

        copies = []
        for number, (at, size) in enumerate(blocks):
            stay = [
                stay_refs[index][pl.ds(first, rows), :]
                for index, first, rows in covering(stay_rows_in, at, size)
            ]
            travel = [
                travel_part(index, first, rows)
                for index, first, rows in covering(travel_rows_in, at, size)
            ]
            both = jnp.concatenate([jnp.concatenate(stay, 0), jnp.concatenate(travel, 0)], 1)
            right = times(both, turn)
            span = pl.ds(at, size)
            if at < head:
                basis_ref[span, :BLOCK] = left_ref[span, :]
                basis_ref[span, BLOCK:] = right
                continue
            whole[span, :BLOCK] = left_ref[span, :]
            whole[span, BLOCK:] = right
            copy = pltpu.make_async_copy(
                whole.at[span, :], out_ref.at[pl.ds(at - head, size), :], sems.at[number]
            )
            copy.start(priority=number % 2)
            copies.append(copy)
        for copy in copies:
            copy.wait()

    return pl.pallas_call(
        body,
        out_shape=(shaped(total - head, 2 * BLOCK), shaped(head, 2 * BLOCK)),
        in_specs=[VMEM] * (2 + count + len(flat)),
        out_specs=(HBM, VMEM),
        scratch_shapes=[
            pltpu.VMEM((total, 2 * BLOCK), jnp.float32),
            pltpu.SemaphoreType.DMA((len(blocks),)),
        ],
        compiler_params=limit(20),
        cost_estimate=cost(6 * total * 256 * 128, 2048 * total),
        name="arriving",
    )(left, turn, *stays, *flat)


def per_device(jacobian, row_weight, col_scale, round_count, move_flag):
    rows, width = jacobian.shape
    move_flag = move_flag.reshape(STEPS)
    weight = row_weight.reshape(rows // BLOCK, BLOCK)
    scale = col_scale.reshape(1, width)
    head = width * lax.axis_size("blk") // lax.axis_size("rows")
    early_count = EARLY + EARLY_MORE
    late = rows - early_count
    cut = (late - head) // 2 // BLOCK * BLOCK
    starts = (0, cut, late)
    sizes = (head + cut, late - cut)
    stay_sizes = (sizes[0] - BLOCK, sizes[1] + BLOCK)
    barrier = lax.optimization_barrier

    early, jacobian = lax.optimization_barrier(
        (early_rows(jacobian, weight, scale, EARLY), jacobian)
    )
    early_near = from_behind(early, "blk", 1)
    scaled, keep, send = gram_of(jacobian, weight, scale)
    more_near = from_behind(rows_of(scaled, late, EARLY_MORE), "blk", 1)
    own, other = sum_pieces(keep, send, "rows")
    own, early_near = barrier((own, early_near))
    stay_turn, travel_turn, piece, gram, w_stay, w_travel = first_rounds(
        round_count, move_flag, own, other, head
    )
    piece = from_behind(piece, "blk", 1)

    go = [
        product(scaled, travel_turn, w_travel, 0, cut, "travel_0"),
        product(scaled, travel_turn, None, cut, late - cut, "travel_1"),
    ]
    go_early = product(scaled, travel_turn, None, late, early_count, "travel_early")
    stay, *stays = stay_rows(scaled, stay_turn, w_stay, stay_sizes)

    near, stays_near = [None] * 2, [None] * 2
    first_odd = hop(go[0], "blk", 1)
    passing, piece, more_near = barrier(
        (passed_on(go[0], first_odd, "pass_0"), piece, more_near)
    )
    near[0] = swap(passing, "blk", 1)
    go[1], first_odd, stay, stays[0], go_early = barrier(
        (go[1], first_odd, stay, stays[0], go_early)
    )
    second = from_behind(go[1], "blk", 2)
    passing, near[0] = barrier((passed_on(go[1], second, "pass_1"), near[0]))
    near[1] = swap(passing, "blk", 1)

    near_early, stay_early, gram_near, cross = near_rows(
        stay, more_near, early_near, gathered(piece, "rows")
    )
    stays[0], cross = barrier((stays[0], cross))
    stay_odd = hop(stays[0], "blk", 1)
    go[0], second = barrier((go[0], second))
    first_even = hop(go[0], "blk", 0)
    passing, near[1] = barrier((passed_on(stays[0], stay_odd, "pass_2"), near[1]))
    stays_near[0] = swap(passing, "blk", 1)
    stays[1], stay_odd = barrier((stays[1], stay_odd))
    stay_odd_two = hop(stays[1], "blk", 1)

    (cross,) = add_cross(stay, near[0], cross, head, head, False)
    keep, send = add_cross(stay, near[1], cross, sizes[0], 0, True)
    keep, send, first_even, go_early = barrier((keep, send, first_even, go_early))
    early_two = from_behind(go_early, "blk", 2)
    own, other = sum_pieces(keep, send, "rows")
    own, stays_near[0] = barrier((own, stays_near[0]))
    stays[1], stay_odd_two, own = barrier((stays[1], stay_odd_two, own))
    stays_near[1] = swap(passed_on(stays[1], stay_odd_two, "pass_3"), "blk", 1)
    stay_next, travel_next = second_rounds(round_count, move_flag, own, other, gram, gram_near)
    turn_near = from_behind(travel_next, "blk", 1)
    left = staying(stay, near + [near_early], stay_next)
    left, early_two = barrier((left, early_two))
    travels = [(first_odd, first_even), second, early_two]
    stays_near.append(stay_early)
    return arriving(left, head, stays_near, travels, turn_near)


def solution(mesh):
    in_specs = (P("rows", "blk"), P("rows"), P("blk"), P(), P(None, "blk"))
    out_specs = (P("rows", "blk"), P("rows", "blk"))
    return jax.shard_map(
        per_device, mesh=mesh, in_specs=in_specs, out_specs=out_specs, check_vma=False
    )
```
